32 devices in a mesh: parts: 2 (over y), dp: 4 (over x, core), fsdp: 4 (over z).
Axes of the slice: x: 2, y: 2, z: 4, core: 2. Of those that a mesh axis runs over, the one named last changes fastest.
Arguments:
- hidden: bfloat16 [16384, 5120], P(('parts', 'dp', 'fsdp')), parts along dimension 0, may hold values from -6 to 6
- queries: bfloat16 [16384, 4096], P(('parts', 'dp', 'fsdp')), parts along dimension 0, may hold values from -180 to 180
- key_matrix: bfloat16 [5120, 512], P('fsdp'), may hold values from -0.078125 to 0.078125
- value_matrix: bfloat16 [5120, 512], P('fsdp'), may hold values from -0.078125 to 0.078125
- key_gain: float32 [128], replicated, may hold values from 0.1 to 1.9
- read_out: float32 [4096], replicated, may hold values from -0.5 to 0.5
- placing: int32 [8, 8], P(('parts', 'fsdp')), parts along dimension 0, may hold values from 0 to 7, as said below
- segments: int32 [16384], P(('parts', 'dp', 'fsdp')), parts along dimension 0, may hold values from 0 to 63, never falling along the last dimension, each value on 1 to 256 neighbouring positions
Outputs:
- head_estimates: float32 [16384, 32], P(('parts', 'dp', 'fsdp')), parts along dimension 0
- estimates: float32 [16384], P(('parts', 'dp', 'fsdp')), parts along dimension 0
The draws below stay inside these ranges and needn't reach their ends.
There are 2 independent parts, one for each index of `parts`. The reference program is written for one: setup_inputs(seed, part) draws one part's arguments, and reference() takes and returns one part's arrays. A program takes and returns all parts, laid end to end along the dimension named above; an argument that names none is the same for every part. Nothing has to cross between parts.
Inputs may be any that keep to these rules, and one draw needn't show every extreme that they name: Each row of placing is a permutation of the packed positions; the 2 blocks of one device always go to 2 different dp ranks (at most 1 block of a device per dp rank). `segments`: segment ids never fall along the tokens; a segment has at most 256 tokens.
All inputs are finite; a program needn't handle non-finite values.
Results may differ from the reference program's by a relative error of at most 0.012.
Values may be sent and summed in bfloat16 or wider, within the bound.
A program may use at most 192 MiB of HBM per device.

```python
import math
import jax
import jax.numpy as jnp
import numpy as np
from jax import lax

MODEL_WIDTH = 5120
QUERY_HEADS = 32
KEY_VALUE_HEADS = 4
HEAD_SIZE = 128
BLK = 256
BPD = 2
TOK_DEV = 512
TOKENS = 8192
N_DP = 4
N_FSDP = 4


def draw_queries(key, part):
    key = jax.random.fold_in(key, 11)
    first = jax.random.fold_in(key, 0)
    shape = (TOKENS, QUERY_HEADS * HEAD_SIZE)
    base = jax.random.normal(first, shape, jnp.float32)
    base = jnp.clip(base, -6.0, 6.0)
    return base.astype(jnp.bfloat16)


def draw_placing(key, part):
    key = jax.random.fold_in(key, 23)

    def column(number):
        column_key = jax.random.fold_in(key, number)
        first, second, third = jax.random.split(column_key, 3)
        ranking = jax.random.permutation(first, N_DP).astype(jnp.int32)
        offset = jax.random.randint(second, (), 0, N_DP, dtype=jnp.int32)
        ordering = jax.random.permutation(third, BPD).astype(jnp.int32)
        device = jnp.arange(N_DP, dtype=jnp.int32)[:, None]
        block = jnp.arange(BPD, dtype=jnp.int32)[None, :]
        target = jnp.take(ranking, (device + offset + block) % N_DP)
        return (target * BPD + jnp.take(ordering, block)).reshape(N_DP * BPD).astype(jnp.int32)
    return jax.vmap(column)(jnp.arange(N_FSDP, dtype=jnp.int32))


def levels(rng, extent, cuts, smallest, top_value):
    def one(position, parts):
        draws = jax.random.uniform(jax.random.fold_in(jax.random.fold_in(rng, 6), position), (parts,), jnp.float32, smallest / len(cuts), top_value / len(cuts))
        return jnp.repeat(jnp.exp(draws), extent[position] // parts).reshape((-1,) + (1,) * (len(extent) - position - 1))

    level = one(*cuts[0])
    for cut in cuts[1:]:
        level = level * one(*cut)
    return level


def length_profile(amount, total, limit, slope):
    weights = [(1 << 20) // math.isqrt(grade ** slope) + 1 for grade in range(2, amount + 1)]
    surplus, counts = total - limit - (amount - 1), [1] * (amount - 1)
    while surplus > 0:
        free = [i for i in range(amount - 1) if counts[i] < limit]
        whole, left = sum([weights[i] for i in free]), surplus
        for i in free:
            addition = min(limit - counts[i], max(1, left * weights[i] // whole), surplus)
            counts[i] = counts[i] + addition
            surplus = surplus - addition
    return np.array([limit] + counts)


def ragged(own_key, count, total, bound, slope):
    if count == 2:
        one = jax.random.randint(own_key, (), max(1, total - bound), min(bound, total - 1) + 1)
        return jnp.stack([one, total - one])
    tallies = jnp.asarray(length_profile(count, total, bound, slope), jnp.int32)
    twos = (count - 1) // 2
    source_of, taker = tallies[1:1 + 2 * twos:2], tallies[2:2 + 2 * twos:2]
    room = jnp.minimum(source_of - 1, bound - taker)
    passed = jax.random.randint(jax.random.fold_in(own_key, 1), (twos,), 0, 1 << 20) % (room + 1)
    tallies = tallies.at[1:1 + 2 * twos:2].set(source_of - passed).at[2:2 + 2 * twos:2].set(taker + passed)
    return tallies[jax.random.permutation(jax.random.fold_in(own_key, 2), count)]


def gaussian(key, shape, spread, reach, cuts=(), kind=jnp.bfloat16):
    array = spread * jax.random.normal(key, shape, jnp.float32)
    if cuts:
        array = array * levels(key, shape, cuts, -0.22, 0.18)
    return jnp.clip(array, -reach, reach).astype(kind)


def setup_inputs(seed: int = 0, part: int = 0) -> dict:
    streams_of = jax.random.split(jax.random.key(seed), 9)
    part_splits = jax.random.split(jax.random.fold_in(streams_of[8], part), 9)
    hidden = gaussian(part_splits[0], (TOKENS, MODEL_WIDTH), 1.0, 6.0, ((0, 16),))
    queries = draw_queries(jax.random.fold_in(jax.random.fold_in(streams_of[8], part), 71), part)
    key_matrix = gaussian(streams_of[2], (MODEL_WIDTH, KEY_VALUE_HEADS * HEAD_SIZE), MODEL_WIDTH ** -0.5, 0.078125, ((0, 4),))
    value_matrix = gaussian(streams_of[3], (MODEL_WIDTH, KEY_VALUE_HEADS * HEAD_SIZE), MODEL_WIDTH ** -0.5, 0.078125, ((0, 4),))
    key_gain = jnp.clip(1.0 + 0.18 * jax.random.normal(streams_of[4], (HEAD_SIZE,), jnp.float32), 0.1, 1.9)
    read_out = gaussian(streams_of[5], (QUERY_HEADS * HEAD_SIZE,), HEAD_SIZE ** -0.5, 0.5, (), jnp.float32)
    placing = draw_placing(jax.random.fold_in(jax.random.fold_in(streams_of[8], part), 71), part)
    segments = jnp.searchsorted(jnp.cumsum(ragged(part_splits[7], TOKENS // (BLK // 2), TOKENS, BLK, 2)), jnp.arange(TOKENS), side="right").astype(jnp.int32)
    return {"hidden": hidden, "queries": queries, "key_matrix": key_matrix, "value_matrix": value_matrix, "key_gain": key_gain, "read_out": read_out, "placing": placing, "segments": segments}


def rms_keys(raw, gain):
    token_rows = raw.shape[0]
    heads = raw.reshape(token_rows, -1, gain.shape[0])
    scale = lax.rsqrt(lax.optimization_barrier(jnp.mean(heads * heads, axis=-1, keepdims=True)) + 1e-06)
    return (heads * scale * gain).astype(jnp.bfloat16).reshape(token_rows, -1)

def relocate(values, index):
    width = values.shape[-1]
    grid = values.reshape(N_DP, N_FSDP, BPD * BLK * width).transpose(1, 0, 2)
    grid = grid.reshape(N_FSDP, N_DP * BPD, BLK * width)
    moved = jnp.take_along_axis(grid, index.astype(jnp.int32)[:, :, None], axis=1)
    moved = moved.reshape(N_FSDP, N_DP, BPD * BLK * width).transpose(1, 0, 2)
    return moved.reshape(-1, width)

def attend(query_tile, key_tile, value_tile, tile_s):
    token_rows = query_tile.shape[0]
    head_group = QUERY_HEADS // KEY_VALUE_HEADS
    query_heads = query_tile.reshape(token_rows, KEY_VALUE_HEADS, head_group, HEAD_SIZE).astype(jnp.float32)
    key_heads = key_tile.reshape(token_rows, KEY_VALUE_HEADS, HEAD_SIZE).astype(jnp.float32)
    value_heads = value_tile.reshape(token_rows, KEY_VALUE_HEADS, HEAD_SIZE).astype(jnp.float32)
    scores = jnp.einsum('agrd,bgd->grab', query_heads, key_heads) / jnp.sqrt(jnp.float32(HEAD_SIZE))
    place = jnp.arange(token_rows, dtype=jnp.int32)
    allowed = (tile_s[:, None] == tile_s[None, :]) & (place[None, :] <= place[:, None])
    scores = jnp.where(allowed, scores, jnp.float32(-1e+30))
    top = lax.optimization_barrier(jnp.max(scores, axis=-1, keepdims=True))
    expo = jnp.where(allowed, jnp.exp(scores - top), jnp.float32(0.0))
    weights = (expo / lax.optimization_barrier(jnp.sum(expo, axis=-1, keepdims=True))).astype(jnp.bfloat16)
    context = jnp.einsum('grab,bgd->agrd', weights.astype(jnp.float32), value_heads)
    return context.reshape(token_rows, QUERY_HEADS * HEAD_SIZE).astype(jnp.bfloat16)

def reference(hidden, queries, key_matrix, value_matrix, key_gain, read_out, placing, segments):
    key_raw = jnp.dot(hidden, key_matrix, preferred_element_type=jnp.float32)
    value_raw = jnp.dot(hidden, value_matrix, preferred_element_type=jnp.float32)
    keys = rms_keys(key_raw, key_gain)
    vals = value_raw.astype(jnp.bfloat16)
    inverse = jnp.argsort(placing, axis=1).astype(jnp.int32)
    packed_q = relocate(queries, inverse)
    packed_k = relocate(keys, inverse)
    packed_v = relocate(vals, inverse)
    tiles = TOKENS // TOK_DEV

    def one(items):
        return attend(items[0], items[1], items[2], items[3])
    packed_context = lax.map(one, (packed_q.reshape(tiles, TOK_DEV, -1), packed_k.reshape(tiles, TOK_DEV, -1), packed_v.reshape(tiles, TOK_DEV, -1), segments.reshape(tiles, TOK_DEV)))
    packed_context = packed_context.reshape(TOKENS, QUERY_HEADS, HEAD_SIZE).astype(jnp.float32)
    head_estimates = lax.optimization_barrier(jnp.sum(packed_context * read_out.reshape(QUERY_HEADS, HEAD_SIZE)[None], axis=-1))
    packed_estimates = lax.optimization_barrier(jnp.sum(head_estimates, axis=1))
    estimates = relocate(packed_estimates[:, None], placing).reshape(TOKENS)
    return (head_estimates, estimates)
```

```python
import math

import jax
import jax.numpy as jnp
from jax import lax
from jax.experimental import pallas as pl
from jax.experimental.pallas import tpu as pltpu
from jax.sharding import PartitionSpec as P

QUERY_HEADS = 32
KEY_VALUE_HEADS = 4
HEAD_SIZE = 128
BLK = 256
GROUP = QUERY_HEADS // KEY_VALUE_HEADS
KEY_WIDTH = KEY_VALUE_HEADS * HEAD_SIZE
NEG = -1e30


def attend_kernel(idx_ref, q_ref, kp_ref, ko_ref, scol_ref, srow_ref, out_ref):
    place_a = lax.broadcasted_iota(jnp.int32, (BLK, BLK), 0)
    place_b = lax.broadcasted_iota(jnp.int32, (BLK, BLK), 1)
    column = scol_ref[0]
    row = srow_ref[0]
    bias_p = jnp.where(column == row[:, :BLK], 0.0, NEG)
    bias_o = jnp.where((column == row[:, BLK:]) & (place_b <= place_a), 0.0, NEG)
    bias = jnp.concatenate([bias_p, bias_o], axis=1)
    lane = lax.broadcasted_iota(jnp.int32, (BLK, HEAD_SIZE), 1)
    both = 2 * BLK
    readout = jnp.concatenate([kp_ref[0, :, KEY_WIDTH:], ko_ref[0, :, KEY_WIDTH:]], axis=0)
    result = jnp.zeros((BLK, HEAD_SIZE), jnp.float32)
    for g in range(KEY_VALUE_HEADS):
        cols = slice(g * HEAD_SIZE, (g + 1) * HEAD_SIZE)
        keys = jnp.concatenate([kp_ref[0, :, cols], ko_ref[0, :, cols]], axis=0)
        for r in range(GROUP):
            h = g * GROUP + r
            q = q_ref[:, h * HEAD_SIZE:(h + 1) * HEAD_SIZE]
            s = lax.dot_general(q, keys, (((1,), (1,)), ((), ())),
                                preferred_element_type=jnp.float32) + bias
            top = jnp.max(s, axis=1, keepdims=True)
            p = jnp.exp2(s - top).astype(jnp.bfloat16)
            o = jnp.dot(p, readout, preferred_element_type=jnp.float32)
            result = jnp.where(lane == h, o / o[:, QUERY_HEADS:QUERY_HEADS + 1], result)
    out_ref[0] = result


def attend(index, queries, keys_all, scol, srow):
    width = keys_all.shape[-1]
    count = scol.shape[0]
    grid_spec = pltpu.PrefetchScalarGridSpec(
        num_scalar_prefetch=1,
        grid=(count,),
        in_specs=[
            pl.BlockSpec((BLK, queries.shape[1]), lambda b, idx: (b, 0)),
            pl.BlockSpec((1, BLK, width), lambda b, idx: (idx[b], 0, 0)),
            pl.BlockSpec((1, BLK, width), lambda b, idx: (idx[count + b], 0, 0)),
            pl.BlockSpec((1, BLK, 1), lambda b, idx: (b, 0, 0)),
            pl.BlockSpec((1, 1, 2 * BLK), lambda b, idx: (b, 0, 0)),
        ],
        out_specs=pl.BlockSpec((1, BLK, HEAD_SIZE), lambda b, idx: (b, 0, 0)),
    )
    return pl.pallas_call(
        attend_kernel,
        grid_spec=grid_spec,
        out_shape=jax.ShapeDtypeStruct((count, BLK, HEAD_SIZE), jnp.float32),
        compiler_params=pltpu.CompilerParams(vmem_limit_bytes=40 * 1024 * 1024),
    )(index, queries, keys_all, keys_all, scol, srow)


def fused_kernel(
    idx_ref, h_hbm, q_hbm, k_ref, v_ref, spread_ref, gain_ref, seg_ref,
    head_ref, est_ref,
    h_buf, q_buf, w_buf, tail_buf, kb0, kb1, kb2, kb3, kb4, seg_buf, bias_buf, res_buf, res_all,
    in_sem, zs, zr, ys, yr, cs, cr, ks, kr, ss, sr, rs, rr,
):
    parts_at = lax.axis_index("parts")
    rank = lax.axis_index("dp")
    z = lax.axis_index("fsdp")
    groups = lax.axis_size("dp")
    n = lax.axis_size("fsdp")
    core = lax.rem(rank, 2)
    sibling = rank + 1 - 2 * core
    other_part = 1 - parts_at
    shard = k_ref.shape[0]
    quarter, half = shard // 4, shard // 2
    kbs = (kb0, kb1, kb2, kb3, kb4)
    chunks = len(kbs)
    count = seg_ref.shape[0]

    def remote(src, dst, send, recv, device):
        return pltpu.make_async_remote_copy(
            src_ref=src, dst_ref=dst, send_sem=send, recv_sem=recv,
            device_id=device, device_id_type=pl.DeviceIdType.MESH)

    load_h = pltpu.make_async_copy(h_hbm, h_buf, in_sem.at[0])
    load_q = pltpu.make_async_copy(q_hbm, q_buf, in_sem.at[1])
    load_h.start()
    load_q.start()

    barrier = pltpu.get_barrier_semaphore()
    peers = [{"parts": parts_at, "dp": rank, "fsdp": lax.rem(z + d, n)} for d in range(1, n)]
    peers += [{"parts": parts_at, "dp": lax.rem(rank + d, groups), "fsdp": z} for d in range(1, groups)]
    peers += [{"parts": other_part, "dp": rank, "fsdp": z}]
    for peer in peers:
        pl.semaphore_signal(barrier, inc=1, device_id=peer, device_id_type=pl.DeviceIdType.MESH)

    high = spread_ref[...].astype(jnp.bfloat16)
    low = (spread_ref[...] - high.astype(jnp.float32)).astype(jnp.bfloat16)
    folded = (jnp.dot(v_ref[...], high, preferred_element_type=jnp.float32)
              + jnp.dot(v_ref[...], low, preferred_element_type=jnp.float32))
    tail_buf[...] = folded.astype(jnp.bfloat16)
    pl.semaphore_wait(barrier, len(peers))

    own_rows = core * half + parts_at * quarter
    peer_rows = core * half + other_part * quarter

    def source(c, first, size):
        if c == 0:
            return tail_buf.at[pl.ds(first, size)]
        return k_ref.at[pl.ds(first, size), pl.ds((c - 1) * HEAD_SIZE, HEAD_SIZE)]

    def behind(d):
        return lax.rem(z - d + n, n)

    def z_copy(c, d):
        return remote(source(c, own_rows, quarter), w_buf.at[c, pl.ds(z * shard + own_rows, quarter)],
                      zs.at[c, d], zr.at[c, d], {"fsdp": lax.rem(z + d, n)})

    def y_copy(c, d):
        at = w_buf.at[c, pl.ds(behind(d) * shard + own_rows, quarter)]
        return remote(at, at, ys.at[c, d], yr.at[c, d], {"parts": other_part})

    def c_copy(c, d):
        at = w_buf.at[c, pl.ds(behind(d) * shard + core * half, half)]
        return remote(at, at, cs.at[c, d], cr.at[c, d], {"dp": sibling})

    def k_copy(c, d):
        at = kbs[c].at[pl.ds(rank * count, count)]
        return remote(at, at, ks.at[c, d], kr.at[c, d], {"dp": lax.rem(rank + d, groups)})

    def s_copy(d):
        return remote(seg_ref, seg_buf.at[pl.ds(rank * count, count)],
                      ss.at[d], sr.at[d], {"dp": lax.rem(rank + d, groups)})

    def r_copy(d):
        at = res_all.at[pl.ds(rank * count, count)]
        return remote(at, at, rs.at[d], rr.at[d], {"dp": lax.rem(rank + d, groups)})

    def start_z(c):
        for d in range(1, n):
            z_copy(c, d).start()

    def pass_y(c):
        for d in range(1, n):
            z_copy(c, d).wait_recv()
            y_copy(c, d).start()

    def pass_core(c):
        for d in range(1, n):
            y_copy(c, d).wait_recv()
            c_copy(c, d).start()

    def project(c):
        for d in range(1, n):
            c_copy(c, d).wait_recv()
        raw = jnp.dot(h_buf[...], w_buf[c], preferred_element_type=jnp.float32)
        if c == 0:
            lane = lax.broadcasted_iota(jnp.int32, raw.shape, 1)
            value = jnp.where(lane == QUERY_HEADS, 1.0, raw)
        else:
            scale = lax.rsqrt(jnp.mean(raw * raw, axis=1, keepdims=True) + 1e-06)
            value = raw * scale * gain_ref[...]
        value = value.astype(jnp.bfloat16)
        for b in range(count):
            kbs[c][rank * count + b] = value[b * BLK:(b + 1) * BLK]
        for d in range(1, groups):
            k_copy(c, d).start()

    def masks():
        for d in range(1, groups):
            s_copy(d).wait_recv()
        place_a = lax.broadcasted_iota(jnp.int32, (BLK, BLK), 0)
        place_b = lax.broadcasted_iota(jnp.int32, (BLK, BLK), 1)
        for b in range(count):
            row = seg_buf[idx_ref[2, b]]
            before = jnp.where(idx_ref[4, b] == 1, seg_buf[idx_ref[3, b]], -1)
            wide = jnp.broadcast_to(row.astype(jnp.float32), (HEAD_SIZE, BLK))
            column = wide.T[:, :1].astype(jnp.int32)
            bias_buf[b, :, :BLK] = jnp.where(column == before, 0.0, NEG)
            bias_buf[b, :, BLK:] = jnp.where((column == row) & (place_b <= place_a), 0.0, NEG)

    def attend_group(c):
        for d in range(1, groups):
            k_copy(c, d).wait_recv()
        lane = lax.broadcasted_iota(jnp.int32, (BLK, HEAD_SIZE), 1)

        def block(b, carry):
            first, second = idx_ref[0, b], idx_ref[1, b]
            readout = jnp.concatenate([kb0[first], kb0[second]], axis=0)
            keys = jnp.concatenate([kbs[c][first], kbs[c][second]], axis=0)
            result = res_buf[b]
            for r in range(GROUP):
                head = (c - 1) * GROUP + r
                q = q_buf[pl.ds(pl.multiple_of(b * BLK, BLK), BLK), head * HEAD_SIZE:(head + 1) * HEAD_SIZE]
                s = lax.dot_general(q, keys, (((1,), (1,)), ((), ())),
                                    preferred_element_type=jnp.float32) + bias_buf[b]
                top = jnp.max(s, axis=1, keepdims=True)
                p = jnp.exp2(s - top).astype(jnp.bfloat16)
                o = jnp.dot(p, readout, preferred_element_type=jnp.float32)
                result = jnp.where(lane == head, o / o[:, QUERY_HEADS:QUERY_HEADS + 1], result)
            res_buf[b] = result
            return carry

        lax.fori_loop(0, count, block, 0)

    start_z(0)
    start_z(1)
    seg_buf[pl.ds(rank * count, count)] = seg_ref[...]
    for d in range(1, groups):
        s_copy(d).start()
    here = pl.multiple_of(z * shard, shard)
    w_buf[0, pl.ds(here, shard)] = tail_buf[...]
    for c in range(1, chunks):
        w_buf[c, pl.ds(here, shard)] = k_ref[:, (c - 1) * HEAD_SIZE:c * HEAD_SIZE]
    res_buf[...] = jnp.zeros_like(res_buf)
    load_h.wait()
    load_q.wait()
    masks()
    for i in range(chunks + 3):
        if i + 2 < chunks:
            start_z(i + 2)
        if i < chunks:
            pass_y(i)
        if 0 <= i - 1 < chunks:
            pass_core(i - 1)
        if 0 <= i - 2 < chunks:
            project(i - 2)
        if i - 3 == 0:
            for d in range(1, groups):
                k_copy(0, d).wait_recv()
        if 1 <= i - 3 < chunks:
            attend_group(i - 3)

    for b in range(count):
        across = res_buf[b].T[:QUERY_HEADS]
        res_all[rank * count + b] = across
        est_ref[b] = jnp.sum(across, axis=0, keepdims=True)
    for d in range(1, groups):
        r_copy(d).start()
    for c in range(chunks):
        for d in range(1, n):
            z_copy(c, d).wait_send()
            y_copy(c, d).wait_send()
            c_copy(c, d).wait_send()
        for d in range(1, groups):
            k_copy(c, d).wait_send()
    for d in range(1, groups):
        s_copy(d).wait_send()
    for d in range(1, groups):
        r_copy(d).wait_recv()
    for b in range(count):
        head_ref[b * BLK:(b + 1) * BLK, :] = res_all[idx_ref[5, b]].T
    for d in range(1, groups):
        r_copy(d).wait_send()


def fused(index, hidden, queries, key_matrix, value_matrix, spread, gain, segments):
    rows, width = hidden.shape
    count = rows // BLK
    n, groups = lax.axis_size("fsdp"), lax.axis_size("dp")
    total = groups * count
    chunks = KEY_VALUE_HEADS + 1
    vmem = pl.BlockSpec(memory_space=pltpu.VMEM)
    anywhere = pl.BlockSpec(memory_space=pl.ANY)
    dma = pltpu.SemaphoreType.DMA
    return pl.pallas_call(
        fused_kernel,
        in_specs=[pl.BlockSpec(memory_space=pltpu.SMEM), anywhere, anywhere, vmem, vmem, vmem, vmem, vmem],
        out_specs=[vmem, vmem],
        out_shape=[
            jax.ShapeDtypeStruct((rows, QUERY_HEADS), jnp.float32),
            jax.ShapeDtypeStruct((count, 1, BLK), jnp.float32),
        ],
        scratch_shapes=[
            pltpu.VMEM((rows, width), jnp.bfloat16),
            pltpu.VMEM(queries.shape, jnp.bfloat16),
            pltpu.VMEM((chunks, width, HEAD_SIZE), jnp.bfloat16),
            pltpu.VMEM((width // n, HEAD_SIZE), jnp.bfloat16),
        ] + [pltpu.VMEM((total, BLK, HEAD_SIZE), jnp.bfloat16)] * chunks + [
            pltpu.VMEM((total, 1, BLK), jnp.int32),
            pltpu.VMEM((count, BLK, 2 * BLK), jnp.float32),
            pltpu.VMEM((count, BLK, HEAD_SIZE), jnp.float32),
            pltpu.VMEM((total, QUERY_HEADS, BLK), jnp.float32),
            dma((2,)),
        ] + [dma((chunks, n))] * 6 + [dma((chunks, groups))] * 2 + [dma((groups,))] * 4,
        compiler_params=pltpu.CompilerParams(
            collective_id=0, has_side_effects=True, vmem_limit_bytes=56 * 1024 * 1024),
        cost_estimate=pl.CostEstimate(flops=10 ** 10, bytes_accessed=2 * 10 ** 7, transcendentals=10 ** 7),
    )(index, hidden, queries, key_matrix, value_matrix, spread, gain, segments)


def per_device(hidden, queries, key_matrix, value_matrix, key_gain, read_out, placing, segments):
    groups = lax.axis_size("dp")
    rank = lax.axis_index("dp")
    rows = hidden.shape[0]
    count = rows // BLK
    total = groups * count
    table = placing[0]
    numbers = jnp.arange(total, dtype=jnp.int32)
    source = jnp.sum(jnp.where(table[None, :] == numbers[:, None], numbers[None, :], 0), axis=1)
    own = rank * count + jnp.arange(count, dtype=jnp.int32)
    packed = jnp.take(table, own)
    odd = (packed % 2) == 1
    partner = jnp.where(odd, jnp.take(source, jnp.maximum(packed - 1, 0)), own)
    head = jnp.arange(QUERY_HEADS)
    spread = jnp.where(
        (head[None, None, :] // GROUP) == jnp.arange(KEY_VALUE_HEADS)[:, None, None],
        read_out.reshape(QUERY_HEADS, HEAD_SIZE).T[None],
        0.0,
    ).reshape(KEY_WIDTH, QUERY_HEADS)
    gain = key_gain * jnp.float32(math.log2(math.e) / math.sqrt(HEAD_SIZE))
    kept = lax.dynamic_slice_in_dim(source, rank * count, count)
    before = jnp.maximum(packed - 1, 0)

    if lax.axis_size("parts") == 2 and groups % 2 == 0 and key_matrix.shape[0] % 64 == 0:
        index = jnp.stack([partner, own, packed, before, odd, kept]).astype(jnp.int32)
        wide = jnp.pad(spread, ((0, 0), (0, HEAD_SIZE - QUERY_HEADS)))
        head_estimates, estimates = fused(
            index, hidden, queries, key_matrix, value_matrix, wide,
            gain.reshape(1, HEAD_SIZE), segments.reshape(count, 1, BLK))
        return (head_estimates, estimates.reshape(rows))

    seg_all = lax.all_gather(segments, "dp", axis=0, tiled=True).reshape(total, BLK)
    seg_own = jnp.take(seg_all, packed, axis=0)
    seg_partner = jnp.take(seg_all, before, axis=0)
    seg_partner = jnp.where(odd[:, None], seg_partner, -1)
    srow = jnp.concatenate([seg_partner, seg_own], axis=1).reshape(count, 1, 2 * BLK)
    scol = seg_own.reshape(count, BLK, 1)

    folded = jnp.dot(value_matrix.astype(jnp.float32), spread, precision=lax.Precision.HIGHEST)
    folded = jnp.pad(folded.astype(jnp.bfloat16), ((0, 0), (0, HEAD_SIZE - QUERY_HEADS)))
    weights = jnp.concatenate([key_matrix, folded], axis=1)
    weights = lax.all_gather(weights, "fsdp", axis=0, tiled=True)
    raw = jnp.dot(hidden, weights, preferred_element_type=jnp.float32)
    heads = raw[:, :KEY_WIDTH].reshape(rows, KEY_VALUE_HEADS, HEAD_SIZE)
    scale = lax.rsqrt(jnp.mean(heads * heads, axis=-1, keepdims=True) + 1e-06)
    keys = (heads * scale * gain).astype(jnp.bfloat16).reshape(rows, KEY_WIDTH)
    lane = jnp.arange(HEAD_SIZE)
    tail = jnp.where(lane[None, :] == QUERY_HEADS, 1.0, raw[:, KEY_WIDTH:]).astype(jnp.bfloat16)
    mine = jnp.concatenate([keys, tail], axis=1)
    everyone = lax.all_gather(mine, "dp", axis=0, tiled=True).reshape(total, BLK, -1)
    index = jnp.concatenate([partner, own]).astype(jnp.int32)
    result = attend(index, queries, everyone, scol, srow)[:, :, :QUERY_HEADS]
    estimates = jnp.sum(result, axis=-1).reshape(rows)
    every_result = lax.all_gather(result, "dp", axis=0, tiled=True)
    head_estimates = jnp.take(every_result, kept, axis=0)
    return (head_estimates.reshape(rows, QUERY_HEADS), estimates)


def solution(mesh):
    in_specs = (
        P(("parts", "dp", "fsdp"), None),
        P(("parts", "dp", "fsdp"), None),
        P("fsdp", None),
        P("fsdp", None),
        P(),
        P(),
        P(("parts", "fsdp"), None),
        P(("parts", "dp", "fsdp")),
    )
    out_specs = (P(("parts", "dp", "fsdp"), None), P(("parts", "dp", "fsdp")))
    return jax.shard_map(
        per_device, mesh=mesh, in_specs=in_specs, out_specs=out_specs, check_vma=False
    )
```
